128 devices in a mesh: row: 8 (over x, z_lo), col: 16 (over y, z_hi, core).
Axes of the slice: x: 4, y: 4, z: 4 (z_hi: 2, z_lo: 2; z = z_hi * 2 + z_lo), core: 2. Of those that a mesh axis runs over, the one named last changes fastest.
Arguments:
- coupling: bfloat16 [3, 256, 65536], P(None, None, ('row', 'col')), may hold values from -6 to 6
- right_coupling: bfloat16 [3, 256, 16384], P(None, None, ('col', 'row')), may hold values from -0.21875 to 0.21875
- upper_inverse: bfloat16 [3, 256, 256], replicated, as said below
- lower_inverse: bfloat16 [3, 256, 256], replicated
- block_mask: int32 [3, 512], P(None, ('row', 'col')), may hold values 0 or 1
- block_map: int32 [512], replicated, may hold values from 0 to 511, as said below
Outputs:
- schur_update: bfloat16 [65536, 16384], P('row', 'col')
The draws below stay inside these ranges and needn't reach their ends.
Inputs may be any that keep to these rules, and one draw needn't show every extreme that they name: upper_inverse[k] is upper triangular and lower_inverse[k] lower triangular, with diagonal entries from 0.5 to 1.5. `block_map`: a permutation of the 512 blocks that keeps each block within its aligned group of 64 blocks.
All inputs are finite; a program needn't handle non-finite values. No bound on the sum of `block_mask` on one device may be relied on, other than what follows from the above.
Results may differ from the reference program's by a relative error of at most 0.0058.
Values may be sent and summed in bfloat16 or wider, within the bound.
No kernel may reach another device: no remote copies, remote signals or barrier semaphores. Data moves between devices by JAX's collectives and lax.ppermute only.
A program may use at most 192 MiB of HBM per device.

```python
import jax
import jax.numpy as jnp
from jax import lax

NI = 65536
PW = 256
PANELS = 3
BW = 128
WC = 16384
NBLK = 512
GBLK = 64
N_ROW = 8
N_COL = 16


def triangular_draw(key, lower):
    off_key = jax.random.fold_in(key, 1)
    diag_key = jax.random.fold_in(key, 2)
    base = jax.random.normal(off_key, (PANELS, PW, PW), jnp.float32) * 0.5 / jnp.sqrt(jnp.float32(PW))
    diagonal = jax.random.uniform(diag_key, (PANELS, PW), jnp.float32, 0.5, 1.5)
    if lower:
        strict = jnp.tril(base, -1)
    else:
        strict = jnp.triu(base, 1)
    return strict + diagonal[:, :, None] * jnp.eye(PW, dtype=jnp.float32)[None, :, :]


def draw_upper_inverse(key, part):
    return triangular_draw(jax.random.fold_in(key, 11), False).astype(jnp.bfloat16)


def draw_lower_inverse(key, part):
    return triangular_draw(jax.random.fold_in(key, 12), True).astype(jnp.bfloat16)


def draw_block_map(key, part):
    groups = NBLK // GBLK
    scores = jax.random.randint(jax.random.fold_in(key, 13), (groups, GBLK), 0, 1024, dtype=jnp.int32)
    scores = scores * GBLK + jnp.arange(GBLK, dtype=jnp.int32)[None, :]
    order = jnp.argsort(scores, axis=1).astype(jnp.int32)
    order = order + (jnp.arange(groups, dtype=jnp.int32) * GBLK)[:, None]
    return order.reshape(NBLK)


def with_ends(values, own_key, smallest, largest):
    place = [jax.random.randint(jax.random.fold_in(own_key, axis), (), 0, length) for axis, length in enumerate(values.shape)]
    longest = values.shape.index(max(values.shape))
    next_to = place[:longest] + [(place[longest] + 1) % values.shape[longest]] + place[longest + 1:]
    return values.at[tuple(place)].set(smallest).at[tuple(next_to)].set(largest)


def level_of(key, shape, cuts, least, high):
    def one(position, blocks):
        heights = jax.random.uniform(jax.random.fold_in(jax.random.fold_in(key, 6), position), (blocks,), jnp.float32, least / len(cuts), high / len(cuts))
        return jnp.repeat(jnp.exp(heights), shape[position] // blocks).reshape((-1,) + (1,) * (len(shape) - position - 1))

    level = one(*cuts[0])
    for cut in cuts[1:]:
        level = level * one(*cut)
    return level


def normal_values(key, shape, spread, reach, shards=(), kind=jnp.bfloat16):
    result = jax.random.normal(key, shape, jnp.float32) * spread
    if len(shards) > 0:
        result = level_of(key, shape, shards, -0.22, 0.18) * result
    return jnp.clip(result, min=-reach, max=reach).astype(kind)


def setup_inputs(seed: int = 0) -> dict:
    key_of = jax.random.split(jax.random.key(seed), 7)
    return {
        "coupling": normal_values(key_of[0], (PANELS, PW, NI), 1.0, 6.0, ((2, 128),)),
        "right_coupling": normal_values(key_of[1], (PANELS, PW, WC), (PANELS * PW) ** -0.5, 0.21875, ((2, 128),)),
        "upper_inverse": draw_upper_inverse(jax.random.fold_in(key_of[6], 71), 0),
        "lower_inverse": draw_lower_inverse(jax.random.fold_in(key_of[6], 71), 0),
        "block_mask": with_ends((jax.random.randint(key_of[4], (PANELS, NBLK), 0, 4) < 3).astype(jnp.int32), jax.random.fold_in(key_of[4], 1), 0, 1),
        "block_map": draw_block_map(jax.random.fold_in(key_of[6], 71), 0),
    }


def reference(coupling, right_coupling, upper_inverse, lower_inverse, block_mask, block_map):
    widened = jnp.repeat(block_mask.astype(jnp.bfloat16), BW, axis=1)
    masked = coupling * widened[:, None, :]
    solved = jnp.einsum("kij,kin->kjn", upper_inverse.astype(jnp.float32), masked.astype(jnp.float32)).astype(jnp.bfloat16)
    devices = N_ROW * N_COL
    piece_cols = NI // (devices * devices)
    relaid = solved.reshape(PANELS, PW, devices, devices, piece_cols).transpose(0, 1, 3, 2, 4).reshape(PANELS, PW, NI)
    mapped = jnp.take(relaid.reshape(PANELS, PW, NBLK, BW), block_map, axis=2).reshape(PANELS, PW, NI)
    right_solved = jnp.einsum("kij,kjn->kin", lower_inverse.astype(jnp.float32), right_coupling.astype(jnp.float32)).astype(jnp.bfloat16)
    right_flat = right_solved.reshape(PANELS * PW, WC)
    left_blocks = mapped.reshape(PANELS * PW, N_ROW, NI // N_ROW).transpose(1, 0, 2)

    def one_block(left_rows):
        product = lax.dot_general(left_rows, right_flat, (((0,), (0,)), ((), ())), preferred_element_type=jnp.float32)
        return (-product).astype(jnp.bfloat16)

    stacked = lax.map(one_block, left_blocks)
    return stacked.reshape(NI, WC)
```

```python
import functools

import jax
import jax.numpy as jnp
from jax import lax
from jax.experimental import pallas as pl
from jax.experimental.pallas import tpu as pltpu
from jax.sharding import PartitionSpec as P

BF = jnp.bfloat16
F32 = jnp.float32
AXES = ("row", "col")
KF = 768
UR = 16
ANY = pl.BlockSpec(memory_space=pl.ANY)
VM = pl.BlockSpec(memory_space=pltpu.VMEM)
SM = pl.BlockSpec(memory_space=pltpu.SMEM)


def coords(d):
    row, col = divmod(d, 16)
    x, zl = divmod(row, 2)
    y, rest = divmod(col, 4)
    zh, core = divmod(rest, 2)
    return x, y, zh * 2 + zl, core


def linear(x, y, z, core):
    x, y, z = x % 4, y % 4, z % 4
    return (x * 2 + z % 2) * 16 + y * 4 + (z // 2) * 2 + core


def permute(a, to):
    return lax.ppermute(a, AXES, [(d, linear(*to(*coords(d)))) for d in range(128)])


def shift(a, dx=0, dy=0, dz=0, dc=0):
    return permute(a, lambda x, y, z, c: (x + dx, y + dy, z + dz, c ^ dc))


R4 = range(4)
XZ = [[linear(x, y, z, c) for x in R4 for z in R4] for y in R4 for c in (0, 1)]
ZZ = [[linear(x, y, z, c) for z in R4] for x in R4 for y in R4 for c in (0, 1)]


def exchange(a, groups):
    return lax.all_to_all(a, AXES, split_axis=0, concat_axis=0, tiled=True, axis_index_groups=groups)


def arr(*shape, dtype=BF):
    return jax.ShapeDtypeStruct(shape, dtype)


def cost(flops, nbytes):
    return pl.CostEstimate(flops=flops, bytes_accessed=nbytes, transcendentals=0)


def place_of(pos):
    row, col = pos[0], pos[1]
    return row // 2, col // 4, (col // 2) % 2 * 2 + row % 2, col % 2


def run(copies):
    for c in copies:
        c.start()
    for c in copies:
        c.wait()


def solve_kernel(pos, mask, coupling, upper, a0, a12, b, c_v, u_v, hold, sem):
    copies = []
    for k in range(3):
        copies.append(pltpu.make_async_copy(coupling.at[k], c_v.at[k], sem.at[k, 0]))
        copies.append(pltpu.make_async_copy(upper.at[k], u_v.at[k], sem.at[k, 1]))
    for c in copies:
        c.start()
    for k in range(3):
        copies[2 * k].wait()
        copies[2 * k + 1].wait()
        row = jnp.concatenate(
            [jnp.broadcast_to(mask[k : k + 1, j : j + 1], (1, 128)) for j in range(4)], axis=1
        )
        masked = c_v[k] * row.astype(F32).astype(BF)
        solved = lax.dot_general(
            masked, u_v[k], (((0,), (0,)), ((), ())), preferred_element_type=F32
        )
        hold[:, :, :, k * 256 : (k + 1) * 256] = solved.astype(BF).reshape(8, 4, UR, 256)
    x, _, z, _ = place_of(pos)
    for to in range(16):
        target = to // 4 * 2 + to % 2
        a0[to] = hold[target, 0]
        a12[to] = hold[target, 1:3]
    for dx in range(4):
        for e in range(2):
            b[dx, e] = hold[lax.rem(x + dx, 4) * 2 + lax.rem(z + e, 2), 3]


def solve(pos, mask, coupling, upper):
    return pl.pallas_call(
        solve_kernel,
        out_shape=(arr(16, UR, KF), arr(16, 2, UR, KF), arr(4, 2, UR, KF)),
        in_specs=[SM, VM, ANY, ANY],
        out_specs=(VM,) * 3,
        scratch_shapes=[
            pltpu.VMEM((3, 256, 512), BF),
            pltpu.VMEM((3, 256, 256), BF),
            pltpu.VMEM((8, 4, UR, KF), BF),
            pltpu.SemaphoreType.DMA((3, 2)),
        ],
        compiler_params=pltpu.CompilerParams(vmem_limit_bytes=16 << 20),
        cost_estimate=cost(2 * 512 * 256 * 768, 4 << 20),
    )(pos, mask, coupling, upper)


def after_y_kernel(pos, own, below, above, far, o0, o1, o2, o3):
    _, y, _, _ = place_of(pos)
    for dy, src in ((0, own), (3, below), (1, above), (2, far)):
        for dx, out in enumerate((o0, o1, o2, o3)):
            out[lax.rem(y + dy, 4)] = src[dx]


def after_y(pos, *parts):
    return pl.pallas_call(
        after_y_kernel,
        out_shape=(arr(4, 2, UR, KF),) * 4,
        in_specs=[SM] + [VM] * 4,
        out_specs=(VM,) * 4,
        compiler_params=pltpu.CompilerParams(vmem_limit_bytes=4 << 20),
        cost_estimate=cost(0, 2 << 20),
    )(pos, *parts)


def after_x_kernel(pos, own, below, above, far, out):
    x, _, z, _ = place_of(pos)
    for dx, src in ((0, own), (3, below), (1, above), (2, far)):
        for dz in range(4):
            for y in range(4):
                out[lax.rem(z + dz, 4), lax.rem(x + dx, 4), y] = src[y, dz % 2]


def after_x(pos, *parts):
    return pl.pallas_call(
        after_x_kernel,
        out_shape=arr(4, 4, 4, UR, KF),
        in_specs=[SM] + [VM] * 4,
        out_specs=VM,
        compiler_params=pltpu.CompilerParams(vmem_limit_bytes=4 << 20),
        cost_estimate=cost(0, 3 << 20),
    )(pos, *parts)


def move_kernel(where, *refs):
    ins, outs = refs[: -len(where)], refs[-len(where) :]
    for out, pieces in zip(outs, where):
        for to, (i, at) in enumerate(pieces):
            out[to] = ins[i][at]


def move(where, shapes, *ins):
    return pl.pallas_call(
        functools.partial(move_kernel, where),
        out_shape=tuple(arr(*s) for s in shapes),
        in_specs=[VM] * len(ins),
        out_specs=(VM,) * len(where),
        compiler_params=pltpu.CompilerParams(vmem_limit_bytes=4 << 20),
        cost_estimate=cost(0, 1 << 20),
    )(*ins)


def halves(below, above):
    where = ([(0, 0), (0, 1)], [(1, 2), (1, 3)])
    return move(where, ((2, 4, UR, KF),) * 2, below, above)


def split(both):
    where = tuple([(0, (i, g)) for i in range(16)] for g in range(2))
    first, second = move(where, ((16, UR, KF),) * 2, both)
    return first.reshape(4, 4, UR, KF), second.reshape(4, 4, UR, KF)


def stack(a, b):
    return move(([(0, ...), (1, ...)],), ((2, KF, 128),), a, b)[0]


def window_kernel(pos, own, below, above, far, lower, out, right):
    x, _, z, _ = place_of(pos)
    for dx, src in ((0, own), (3, below), (1, above), (2, far)):
        for e in range(2):
            r = lax.rem(x + dx, 4) * 2 + lax.rem(z + e, 2)
            right[:, pl.ds(pl.multiple_of(r * 128, 128), 128)] = src[e]
    for k in range(3):
        rows = slice(k * 256, (k + 1) * 256)
        solved = jnp.dot(lower[k], right[rows], preferred_element_type=F32)
        out[rows] = (-solved).astype(BF)


def window(pos, parts, lower):
    return pl.pallas_call(
        window_kernel,
        out_shape=arr(KF, 1024),
        in_specs=[SM] + [VM] * 5,
        out_specs=VM,
        scratch_shapes=[pltpu.VMEM((KF, 1024), BF)],
        compiler_params=pltpu.CompilerParams(vmem_limit_bytes=16 << 20),
        cost_estimate=cost(2 * 768 * 256 * 1024, 4 << 20),
    )(pos, *parts, lower)


def contract_kernel(group, z_major, n_mine, has_base, *refs):
    pos, place, right = refs[:3]
    parts = refs[3 : 3 + 2 * n_mine]
    out, left, stage, out_sem = refs[-4:]
    _, y0, _, core = place_of(pos)

    def fill(u):
        for whose, mine in ((core, parts[:n_mine]), (1 - core, parts[n_mine:])):
            if z_major:
                for z in range(4):
                    left[u % 2, whose, z] = mine[0][z, u]
            else:
                own, below, above, far_low, far_high = mine
                left[u % 2, whose, y0] = own[u]
                left[u % 2, whose, lax.rem(y0 + 3, 4)] = below[u]
                left[u % 2, whose, lax.rem(y0 + 1, 4)] = above[u]
                far = far_low[u] if u < 2 else far_high[u - 2]
                left[u % 2, whose, lax.rem(y0 + 2, 4)] = far

    def stores(u):
        made = []
        for p in range(4):
            at = place[(group * 4 + p) * 4 + u]
            rows = pl.ds(pl.multiple_of(at * 128, 128), 128)
            made.append(pltpu.make_async_copy(stage.at[u % 2, p], out.at[rows], out_sem.at[u % 2, p]))
        return made

    low = lax.broadcasted_iota(jnp.int32, (1, 1, 8, 256), 2) < 4
    for u in range(4):
        fill(u)
        if u >= 2:
            for c in stores(u - 2):
                c.wait()
        flat = left[u % 2].reshape(512, KF)
        for j in range(4):
            cols = slice(j * 256, (j + 1) * 256)
            acc = jnp.dot(flat, right[:, cols], preferred_element_type=F32)
            acc = acc.reshape(2, 16, 2, 8, 256)
            c0, c1 = acc[0], acc[1]
            even = jnp.where(low, c0, pltpu.roll(c1, 4, 2))
            odd = jnp.where(low, pltpu.roll(c0, 4, 2), c1)
            for half, made in enumerate((even, odd)):
                for pair in range(2):
                    for y in range(4):
                        for zl in range(2):
                            at = [
                                made[z * 4 + y if z_major else y * 4 + z, pair]
                                for z in (zl, zl + 2)
                            ]
                            r0 = (zl * 4 + y) * 16
                            stage[u % 2, pair * 2 + half, r0 : r0 + 16, cols] = (
                                jnp.concatenate(at, axis=0).astype(BF)
                            )
        for c in stores(u):
            c.start()
    for u in (2, 3):
        for c in stores(u):
            c.wait()


def contract(group, z_major, pos, place, right, mine, other, base):
    ins = [pos, place, right, *mine, *other]
    specs = [SM, SM] + [VM] * (len(ins) - 2)
    if base is not None:
        ins.append(base)
        specs.append(ANY)
    rows = 4 * 512
    return pl.pallas_call(
        functools.partial(contract_kernel, group, z_major, len(mine), base is not None),
        out_shape=arr(8192, 1024),
        in_specs=specs,
        out_specs=ANY,
        scratch_shapes=[
            pltpu.VMEM((2, 2, 4, 4, UR, KF), BF),
            pltpu.VMEM((2, 4, 128, 1024), BF),
            pltpu.SemaphoreType.DMA((2, 4)),
        ],
        input_output_aliases={} if base is None else {len(ins) - 1: 0},
        compiler_params=pltpu.CompilerParams(vmem_limit_bytes=14 << 20),
        cost_estimate=cost(2 * rows * KF * 1024, rows * (KF + 1024) * 2),
    )(*ins)


def after(value, *done):
    return lax.optimization_barrier((value, *done))[0]


def forward(own, below, above):
    low, high = halves(below, above)
    return [own, below, above, shift(low, dy=1), shift(high, dy=-1)]


def local(coupling, right_coupling, upper_inverse, lower_inverse, block_mask, block_map):
    row, col = lax.axis_index("row"), lax.axis_index("col")
    pos = jnp.stack([row, col]).astype(jnp.int32)

    here = lax.dynamic_slice_in_dim(block_map, row * 64, 64) - row * 64
    slots = jnp.arange(64, dtype=jnp.int32)
    place = jnp.sum(
        jnp.where(here[None, :] == slots[:, None], slots[None, :], 0), axis=1, dtype=jnp.int32
    )

    coupling, place = lax.optimization_barrier((coupling, place))

    a0, a12, b = solve(pos, block_mask, coupling, upper_inverse)
    raw = right_coupling.reshape(KF, 128)
    b_below, b_above, b_far = shift(b, dy=1), shift(b, dy=-1), shift(b, dy=2)
    w_other = permute(raw, lambda x, y, z, c: (x, y, z ^ 1, c))
    s0 = exchange(a0, XZ).reshape(4, 4, UR, KF)

    a12 = after(a12, b_below, b_above, b_far, w_other, s0)
    s12 = exchange(a12, XZ)
    g0, g1, g2, g3 = after_y(pos, b, b_below, b_above, b_far)
    x_below, x_above, x_far = shift(g1, dx=1), shift(g3, dx=-1), shift(g2, dx=2)
    below0, above0 = shift(s0, dy=1), shift(s0, dy=-1)

    bz = after_x(pos, g0, x_below, x_above, x_far)
    s12, bz, below0, above0 = lax.optimization_barrier((s12, bz, below0, above0))
    mine3 = [exchange(bz, ZZ)]
    s1, s2 = split(s12)
    mine0 = forward(s0, below0, above0)

    pair = after(stack(raw, w_other), x_below, x_above, x_far)
    w_below, w_above = shift(pair, dx=1), shift(pair, dx=-1)
    w_far = shift(after(pair, w_below, w_above), dx=2)
    right = window(pos, [pair, w_below, w_above, w_far], lower_inverse)

    s1 = after(s1, below0, above0)
    below1, above1 = shift(s1, dy=1), shift(s1, dy=-1)
    mine1 = forward(s1, below1, above1)
    s2 = after(s2, below1, above1)
    below2, above2 = shift(s2, dy=1), shift(s2, dy=-1)
    mine2 = forward(s2, below2, above2)

    def swapped(mine):
        return [shift(m, dc=1) for m in mine]

    out = contract(0, False, pos, place, right, mine0, swapped(mine0), None)
    out = contract(1, False, pos, place, right, mine1, swapped(mine1), out)
    out = contract(3, True, pos, place, right, mine3, swapped(mine3), out)
    return contract(2, False, pos, place, right, mine2, swapped(mine2), out)


def solution(mesh):
    placed = (
        P(None, None, ("row", "col")),
        P(None, None, ("col", "row")),
        P(),
        P(),
        P(None, ("row", "col")),
        P(),
    )
    return jax.shard_map(
        local, mesh=mesh, in_specs=placed, out_specs=P("row", "col"), check_vma=False
    )
```

```python
import functools

import jax
import jax.numpy as jnp
from jax import lax
from jax.experimental import pallas as pl
from jax.experimental.pallas import tpu as pltpu
from jax.sharding import PartitionSpec as P

BF = jnp.bfloat16
F32 = jnp.float32
AXES = ("row", "col")
KF = 768
DEPTH = 3
UR = 16
ANY = pl.BlockSpec(memory_space=pl.ANY)
VM = pl.BlockSpec(memory_space=pltpu.VMEM)
SM = pl.BlockSpec(memory_space=pltpu.SMEM)


def coords(d):
    row, col = divmod(d, 16)
    x, zl = divmod(row, 2)
    y, rest = divmod(col, 4)
    zh, core = divmod(rest, 2)
    return x, y, zh * 2 + zl, core


def linear(x, y, z, core):
    x, y, z = x % 4, y % 4, z % 4
    return (x * 2 + z % 2) * 16 + y * 4 + (z // 2) * 2 + core


def permute(a, to):
    return lax.ppermute(a, AXES, [(d, linear(*to(*coords(d)))) for d in range(128)])


def shift(a, dx=0, dy=0, dz=0, dc=0):
    return permute(a, lambda x, y, z, c: (x + dx, y + dy, z + dz, c ^ dc))


R4 = range(4)
XZ = [[linear(x, y, z, c) for x in R4 for z in R4] for y in R4 for c in (0, 1)]
XX = [[linear(x, y, z, c) for x in R4] for y in R4 for z in R4 for c in (0, 1)]
YC = [[y * 4 + zh * 2 + c for y in R4 for c in (0, 1)] for zh in (0, 1)]
ZZ = [[linear(x, y, z, c) for z in R4] for x in R4 for y in R4 for c in (0, 1)]


def exchange(a, groups):
    return lax.all_to_all(a, AXES, split_axis=0, concat_axis=0, tiled=True, axis_index_groups=groups)


def arr(*shape, dtype=BF):
    return jax.ShapeDtypeStruct(shape, dtype)


def cost(flops, nbytes):
    return pl.CostEstimate(flops=flops, bytes_accessed=nbytes, transcendentals=0)


def place_of(pos):
    row, col = pos[0], pos[1]
    return row // 2, col // 4, (col // 2) % 2 * 2 + row % 2, col % 2


def run(copies):
    for c in copies:
        c.start()
    for c in copies:
        c.wait()


def solve_kernel(pos, mask, coupling, upper, a, b, c_v, u_v, hold, sem):
    copies = []
    for k in range(3):
        copies.append(pltpu.make_async_copy(coupling.at[k], c_v.at[k], sem.at[k, 0]))
        copies.append(pltpu.make_async_copy(upper.at[k], u_v.at[k], sem.at[k, 1]))
    for c in copies:
        c.start()
    for k in range(3):
        copies[2 * k].wait()
        copies[2 * k + 1].wait()
        row = jnp.concatenate(
            [jnp.broadcast_to(mask[k : k + 1, j : j + 1], (1, 128)) for j in range(4)], axis=1
        )
        masked = c_v[k] * row.astype(F32).astype(BF)
        solved = lax.dot_general(
            masked, u_v[k], (((0,), (0,)), ((), ())), preferred_element_type=F32
        )
        hold[:, :, :, k * 256 : (k + 1) * 256] = solved.astype(BF).reshape(8, 4, UR, 256)
    x, _, z, _ = place_of(pos)
    for to in range(16):
        target = to // 4 * 2 + to % 2
        a[to] = hold[target, 0:3]
    for dx in range(4):
        for e in range(2):
            b[dx, e] = hold[lax.rem(x + dx, 4) * 2 + lax.rem(z + e, 2), 3]


def solve(pos, mask, coupling, upper):
    return pl.pallas_call(
        solve_kernel,
        out_shape=(arr(16, 3, UR, KF), arr(4, 2, UR, KF)),
        in_specs=[SM, VM, ANY, ANY],
        out_specs=(VM,) * 2,
        scratch_shapes=[
            pltpu.VMEM((3, 256, 512), BF),
            pltpu.VMEM((3, 256, 256), BF),
            pltpu.VMEM((8, 4, UR, KF), BF),
            pltpu.SemaphoreType.DMA((3, 2)),
        ],
        compiler_params=pltpu.CompilerParams(vmem_limit_bytes=60 << 20),
        cost_estimate=cost(2 * 512 * 256 * 768, 4 << 20),
    )(pos, mask, coupling, upper)


def after_y_kernel(pos, own, below, above, far, out):
    x, y, _, _ = place_of(pos)
    for dy, src in ((0, own), (3, below), (1, above), (2, far)):
        for dx in range(4):
            out[lax.rem(x + dx, 4), lax.rem(y + dy, 4)] = src[dx]


def after_y(pos, *parts):
    return pl.pallas_call(
        after_y_kernel,
        out_shape=arr(4, 4, 2, UR, KF),
        in_specs=[SM] + [VM] * 4,
        out_specs=VM,
        compiler_params=pltpu.CompilerParams(vmem_limit_bytes=4 << 20),
        cost_estimate=cost(0, 2 << 20),
    )(pos, *parts)


def after_x_kernel(pos, got, out):
    _, _, z, _ = place_of(pos)
    for x in range(4):
        for dz in range(4):
            for y in range(4):
                out[lax.rem(z + dz, 4), x, y] = got[x, y, dz % 2]


def after_x(pos, got):
    return pl.pallas_call(
        after_x_kernel,
        out_shape=arr(4, 4, 4, UR, KF),
        in_specs=[SM, VM],
        out_specs=VM,
        compiler_params=pltpu.CompilerParams(vmem_limit_bytes=4 << 20),
        cost_estimate=cost(0, 3 << 20),
    )(pos, got)


def move_kernel(where, *refs):
    ins, outs = refs[: -len(where)], refs[-len(where) :]
    for out, pieces in zip(outs, where):
        for to, (i, at) in enumerate(pieces):
            out[to] = ins[i][at]


def move(where, shapes, *ins):
    return pl.pallas_call(
        functools.partial(move_kernel, where),
        out_shape=tuple(arr(*s) for s in shapes),
        in_specs=[VM] * len(ins),
        out_specs=(VM,) * len(where),
        compiler_params=pltpu.CompilerParams(vmem_limit_bytes=4 << 20),
        cost_estimate=cost(0, 1 << 20),
    )(*ins)


def stack(a, b):
    return move(([(0, ...), (1, ...)],), ((2, KF, 128),), a, b)[0]


def window_kernel(pos, own, below, above, far, lower, out, right):
    x, _, z, _ = place_of(pos)
    for dx, src in ((0, own), (3, below), (1, above), (2, far)):
        for e in range(2):
            r = lax.rem(x + dx, 4) * 2 + lax.rem(z + e, 2)
            right[:, pl.ds(pl.multiple_of(r * 128, 128), 128)] = src[e]
    for k in range(3):
        rows = slice(k * 256, (k + 1) * 256)
        solved = jnp.dot(lower[k], right[rows], preferred_element_type=F32)
        out[rows] = (-solved).astype(BF)


def window(pos, parts, lower):
    return pl.pallas_call(
        window_kernel,
        out_shape=arr(KF, 1024),
        in_specs=[SM] + [VM] * 5,
        out_specs=VM,
        scratch_shapes=[pltpu.VMEM((KF, 1024), BF)],
        compiler_params=pltpu.CompilerParams(vmem_limit_bytes=16 << 20),
        cost_estimate=cost(2 * 768 * 256 * 1024, 4 << 20),
    )(pos, *parts, lower)


def contract_kernel(groups, gathered, *refs):
    pos, place, right = refs[:3]
    out, right_v, left, stage, r_sem, in_sem, out_sem = refs[-7:]
    _, _, _, core = place_of(pos)
    right_in = pltpu.make_async_copy(right, right_v, r_sem)
    units = [(u, i) for u in range(4) for i in range(len(groups))]

    def loads(n):
        u, i = units[n]
        if gathered:
            pairs = [(refs[3].at[:, u, :, i], left.at[n])]
        else:
            pairs = [
                (refs[3].at[:, u], left.at[n, pl.ds(core * 4, 4)]),
                (refs[4].at[:, u], left.at[n, pl.ds((1 - core) * 4, 4)]),
            ]
        return [
            pltpu.make_async_copy(src, dst, in_sem.at[n, k]) for k, (src, dst) in enumerate(pairs)
        ]

    def stores(n):
        u, i = units[n]
        made = []
        for p in range(4):
            at = place[(groups[i] * 4 + p) * 4 + u]
            rows = pl.ds(pl.multiple_of(at * 128, 128), 128)
            made.append(pltpu.make_async_copy(stage.at[n % 2, p], out.at[rows], out_sem.at[n % 2, p]))
        return made

    for c in loads(0):
        c.start()
    right_in.start()
    for n in range(1, DEPTH):
        for c in loads(n):
            c.start()
    right_in.wait()
    low = lax.broadcasted_iota(jnp.int32, (1, 1, 8, 256), 2) < 4
    for n in range(len(units)):
        for c in loads(n):
            c.wait()
        if n + DEPTH < len(units):
            for c in loads(n + DEPTH):
                c.start()
        if n >= 2:
            for c in stores(n - 2):
                c.wait()
        flat = left[n].reshape(512, KF)
        for j in range(4):
            cols = slice(j * 256, (j + 1) * 256)
            acc = jnp.dot(flat, right_v[:, cols], preferred_element_type=F32)
            if gathered:
                acc = acc.reshape(4, 2, 4, 2, 8, 256)
                c0, c1 = acc[:, 0].reshape(16, 2, 8, 256), acc[:, 1].reshape(16, 2, 8, 256)
            else:
                acc = acc.reshape(2, 16, 2, 8, 256)
                c0, c1 = acc[0], acc[1]
            even = jnp.where(low, c0, pltpu.roll(c1, 4, 2))
            odd = jnp.where(low, pltpu.roll(c0, 4, 2), c1)
            for half, made in enumerate((even, odd)):
                for pair in range(2):
                    for y in range(4):
                        for zl in range(2):
                            at = [
                                made[y * 4 + z if gathered else z * 4 + y, pair]
                                for z in (zl, zl + 2)
                            ]
                            r0 = (zl * 4 + y) * 16
                            stage[n % 2, pair * 2 + half, r0 : r0 + 16, cols] = (
                                jnp.concatenate(at, axis=0).astype(BF)
                            )
        for c in stores(n):
            c.start()
    for n in range(len(units) - 2, len(units)):
        for c in stores(n):
            c.wait()


def contract(groups, gathered, pos, place, right, parts, base):
    ins = [pos, place, right, *parts]
    if base is not None:
        ins.append(base)
    units = 4 * len(groups)
    return pl.pallas_call(
        functools.partial(contract_kernel, groups, gathered),
        out_shape=arr(8192, 1024),
        in_specs=[SM, SM] + [ANY] * (len(ins) - 2),
        out_specs=ANY,
        scratch_shapes=[
            pltpu.VMEM((KF, 1024), BF),
            pltpu.VMEM((units, 8, 4, UR, KF), BF),
            pltpu.VMEM((2, 4, 128, 1024), BF),
            pltpu.SemaphoreType.DMA,
            pltpu.SemaphoreType.DMA((units, 2)),
            pltpu.SemaphoreType.DMA((2, 4)),
        ],
        input_output_aliases={} if base is None else {len(ins) - 1: 0},
        compiler_params=pltpu.CompilerParams(vmem_limit_bytes=56 << 20),
        cost_estimate=cost(2 * units * 512 * KF * 1024, units * 512 * (KF + 1024) * 2),
    )(*ins)


def after(value, *done):
    return lax.optimization_barrier((value, *done))[0]


def local(coupling, right_coupling, upper_inverse, lower_inverse, block_mask, block_map):
    row, col = lax.axis_index("row"), lax.axis_index("col")
    pos = jnp.stack([row, col]).astype(jnp.int32)

    here = lax.dynamic_slice_in_dim(block_map, row * 64, 64) - row * 64
    slots = jnp.arange(64, dtype=jnp.int32)
    place = jnp.sum(
        jnp.where(here[None, :] == slots[:, None], slots[None, :], 0), axis=1, dtype=jnp.int32
    )

    a, b = solve(pos, block_mask, coupling, upper_inverse)
    b_below, b_above, b_far = shift(b, dy=1), shift(b, dy=-1), shift(b, dy=2)
    own, b_below, b_above, b_far = lax.optimization_barrier(
        (exchange(a, XZ).reshape(4, 4, 3, UR, KF), b_below, b_above, b_far)
    )

    whole = lax.all_gather(own, "col", axis=0, tiled=False, axis_index_groups=YC)
    raw = after(right_coupling.reshape(KF, 128), own)
    w_other = permute(raw, lambda x, y, z, c: (x, y, z ^ 1, c))
    by = after_y(pos, b, b_below, b_above, b_far)
    bx, w_other = lax.optimization_barrier((exchange(by, XX), w_other))
    pair = stack(raw, w_other)
    bz, pair = lax.optimization_barrier((after_x(pos, bx), pair))
    zs = exchange(bz, ZZ)
    w_below, w_above, w_far = shift(pair, dx=1), shift(pair, dx=-1), shift(pair, dx=2)
    zs, w_below, w_above, w_far = lax.optimization_barrier((zs, w_below, w_above, w_far))
    right = window(pos, [pair, w_below, w_above, w_far], lower_inverse)
    out = contract((3,), False, pos, place, right, [zs, shift(zs, dc=1)], None)
    return contract((0, 1, 2), True, pos, place, right, [whole], out)


def solution(mesh):
    placed = (
        P(None, None, ("row", "col")),
        P(None, None, ("col", "row")),
        P(),
        P(),
        P(None, ("row", "col")),
        P(),
    )
    return jax.shard_map(
        local, mesh=mesh, in_specs=placed, out_specs=P("row", "col"), check_vma=False
    )
```

```python
import functools

import jax
import jax.numpy as jnp
from jax import lax
from jax.experimental import pallas as pl
from jax.experimental.pallas import tpu as pltpu
from jax.sharding import PartitionSpec as P

BF = jnp.bfloat16
F32 = jnp.float32
AXES = ("row", "col")
KF = 768
DEPTH = 3
UR = 16
ANY = pl.BlockSpec(memory_space=pl.ANY)
VM = pl.BlockSpec(memory_space=pltpu.VMEM)
SM = pl.BlockSpec(memory_space=pltpu.SMEM)


def coords(d):
    row, col = divmod(d, 16)
    x, zl = divmod(row, 2)
    y, rest = divmod(col, 4)
    zh, core = divmod(rest, 2)
    return x, y, zh * 2 + zl, core


def linear(x, y, z, core):
    x, y, z = x % 4, y % 4, z % 4
    return (x * 2 + z % 2) * 16 + y * 4 + (z // 2) * 2 + core


def permute(a, to):
    return lax.ppermute(a, AXES, [(d, linear(*to(*coords(d)))) for d in range(128)])


def shift(a, dx=0, dy=0, dz=0, dc=0):
    return permute(a, lambda x, y, z, c: (x + dx, y + dy, z + dz, c ^ dc))


R4 = range(4)
XZ = [[linear(x, y, z, c) for x in R4 for z in R4] for y in R4 for c in (0, 1)]
XX = [[linear(x, y, z, c) for x in R4] for y in R4 for z in R4 for c in (0, 1)]
YC = [[y * 4 + zh * 2 + c for y in R4 for c in (0, 1)] for zh in (0, 1)]
ZZ = [[linear(x, y, z, c) for z in R4] for x in R4 for y in R4 for c in (0, 1)]


def exchange(a, groups):
    return lax.all_to_all(a, AXES, split_axis=0, concat_axis=0, tiled=True, axis_index_groups=groups)


def arr(*shape, dtype=BF):
    return jax.ShapeDtypeStruct(shape, dtype)


def cost(flops, nbytes):
    return pl.CostEstimate(flops=flops, bytes_accessed=nbytes, transcendentals=0)


def place_of(pos):
    row, col = pos[0], pos[1]
    return row // 2, col // 4, (col // 2) % 2 * 2 + row % 2, col % 2


def run(copies):
    for c in copies:
        c.start()
    for c in copies:
        c.wait()


def solve_kernel(mask, coupling, upper, a, b, c_v, u_v, hold, sem):
    copies = []
    for k in range(3):
        copies.append(pltpu.make_async_copy(coupling.at[k], c_v.at[k], sem.at[k, 0]))
        copies.append(pltpu.make_async_copy(upper.at[k], u_v.at[k], sem.at[k, 1]))
    for c in copies:
        c.start()
    for k in range(3):
        copies[2 * k].wait()
        copies[2 * k + 1].wait()
        row = jnp.concatenate(
            [jnp.broadcast_to(mask[k : k + 1, j : j + 1], (1, 128)) for j in range(4)], axis=1
        )
        masked = c_v[k] * row.astype(F32).astype(BF)
        solved = lax.dot_general(
            masked, u_v[k], (((0,), (0,)), ((), ())), preferred_element_type=F32
        )
        hold[:, :, :, k * 256 : (k + 1) * 256] = solved.astype(BF).reshape(8, 4, UR, 256)
    for to in range(16):
        target = to // 4 * 2 + to % 2
        a[to] = hold[target, 0:3]
    for x in range(4):
        for zl in range(2):
            b[x, zl] = hold[x * 2 + zl, 3]


def solve(mask, coupling, upper):
    return pl.pallas_call(
        solve_kernel,
        out_shape=(arr(16, 3, UR, KF), arr(4, 2, UR, KF)),
        in_specs=[VM, ANY, ANY],
        out_specs=(VM,) * 2,
        scratch_shapes=[
            pltpu.VMEM((3, 256, 512), BF),
            pltpu.VMEM((3, 256, 256), BF),
            pltpu.VMEM((8, 4, UR, KF), BF),
            pltpu.SemaphoreType.DMA((3, 2)),
        ],
        compiler_params=pltpu.CompilerParams(vmem_limit_bytes=60 << 20),
        cost_estimate=cost(2 * 512 * 256 * 768, 4 << 20),
    )(mask, coupling, upper)


def after_y_kernel(pos, own, below, above, far, out):
    _, y, _, _ = place_of(pos)
    for dy, src in ((0, own), (3, below), (1, above), (2, far)):
        for x in range(4):
            out[x, lax.rem(y + dy, 4)] = src[x]


def after_y(pos, *parts):
    return pl.pallas_call(
        after_y_kernel,
        out_shape=arr(4, 4, 2, UR, KF),
        in_specs=[SM] + [VM] * 4,
        out_specs=VM,
        compiler_params=pltpu.CompilerParams(vmem_limit_bytes=4 << 20),
        cost_estimate=cost(0, 2 << 20),
    )(pos, *parts)


def after_x_kernel(got, out):
    for z in range(4):
        for x in range(4):
            for y in range(4):
                out[z, x, y] = got[x, y, z % 2]


def after_x(got):
    return pl.pallas_call(
        after_x_kernel,
        out_shape=arr(4, 4, 4, UR, KF),
        in_specs=[VM],
        out_specs=VM,
        compiler_params=pltpu.CompilerParams(vmem_limit_bytes=4 << 20),
        cost_estimate=cost(0, 3 << 20),
    )(got)


def move_kernel(where, *refs):
    ins, outs = refs[: -len(where)], refs[-len(where) :]
    for out, pieces in zip(outs, where):
        for to, (i, at) in enumerate(pieces):
            out[to] = ins[i][at]


def move(where, shapes, *ins):
    return pl.pallas_call(
        functools.partial(move_kernel, where),
        out_shape=tuple(arr(*s) for s in shapes),
        in_specs=[VM] * len(ins),
        out_specs=(VM,) * len(where),
        compiler_params=pltpu.CompilerParams(vmem_limit_bytes=4 << 20),
        cost_estimate=cost(0, 1 << 20),
    )(*ins)


def stack(a, b):
    return move(([(0, ...), (1, ...)],), ((2, KF, 128),), a, b)[0]


def window_kernel(pos, own, below, above, far, lower, out, right):
    x, _, z, _ = place_of(pos)
    for dx, src in ((0, own), (3, below), (1, above), (2, far)):
        for e in range(2):
            r = lax.rem(x + dx, 4) * 2 + lax.rem(z + e, 2)
            right[:, pl.ds(pl.multiple_of(r * 128, 128), 128)] = src[e]
    for k in range(3):
        rows = slice(k * 256, (k + 1) * 256)
        solved = jnp.dot(lower[k], right[rows], preferred_element_type=F32)
        out[rows] = (-solved).astype(BF)


def window(pos, parts, lower):
    return pl.pallas_call(
        window_kernel,
        out_shape=arr(KF, 1024),
        in_specs=[SM] + [VM] * 5,
        out_specs=VM,
        scratch_shapes=[pltpu.VMEM((KF, 1024), BF)],
        compiler_params=pltpu.CompilerParams(vmem_limit_bytes=16 << 20),
        cost_estimate=cost(2 * 768 * 256 * 1024, 4 << 20),
    )(pos, *parts, lower)


def contract_kernel(groups, gathered, *refs):
    pos, place, right = refs[:3]
    out, right_v, left, stage, r_sem, in_sem, out_sem = refs[-7:]
    _, _, _, core = place_of(pos)
    right_in = pltpu.make_async_copy(right, right_v, r_sem)
    units = [(u, i) for u in range(4) for i in range(len(groups))]

    def loads(n):
        u, i = units[n]
        if gathered:
            pairs = [(refs[3].at[:, u, :, i], left.at[n])]
        else:
            pairs = [
                (refs[3].at[:, u], left.at[n, pl.ds(core * 4, 4)]),
                (refs[4].at[:, u], left.at[n, pl.ds((1 - core) * 4, 4)]),
            ]
        return [
            pltpu.make_async_copy(src, dst, in_sem.at[n, k]) for k, (src, dst) in enumerate(pairs)
        ]

    def stores(n):
        u, i = units[n]
        made = []
        for p in range(4):
            at = place[(groups[i] * 4 + p) * 4 + u]
            rows = pl.ds(pl.multiple_of(at * 128, 128), 128)
            made.append(pltpu.make_async_copy(stage.at[n % 2, p], out.at[rows], out_sem.at[n % 2, p]))
        return made

    for c in loads(0):
        c.start()
    right_in.start()
    for n in range(1, DEPTH):
        for c in loads(n):
            c.start()
    right_in.wait()
    low = lax.broadcasted_iota(jnp.int32, (1, 1, 8, 256), 2) < 4
    for n in range(len(units)):
        for c in loads(n):
            c.wait()
        if n + DEPTH < len(units):
            for c in loads(n + DEPTH):
                c.start()
        if n >= 2:
            for c in stores(n - 2):
                c.wait()
        flat = left[n].reshape(512, KF)
        for j in range(4):
            cols = slice(j * 256, (j + 1) * 256)
            acc = jnp.dot(flat, right_v[:, cols], preferred_element_type=F32)
            if gathered:
                acc = acc.reshape(4, 2, 4, 2, 8, 256)
                c0, c1 = acc[:, 0].reshape(16, 2, 8, 256), acc[:, 1].reshape(16, 2, 8, 256)
            else:
                acc = acc.reshape(2, 16, 2, 8, 256)
                c0, c1 = acc[0], acc[1]
            even = jnp.where(low, c0, pltpu.roll(c1, 4, 2))
            odd = jnp.where(low, pltpu.roll(c0, 4, 2), c1)
            for half, made in enumerate((even, odd)):
                for pair in range(2):
                    for y in range(4):
                        for zl in range(2):
                            at = [
                                made[y * 4 + z if gathered else z * 4 + y, pair]
                                for z in (zl, zl + 2)
                            ]
                            r0 = (zl * 4 + y) * 16
                            stage[n % 2, pair * 2 + half, r0 : r0 + 16, cols] = (
                                jnp.concatenate(at, axis=0).astype(BF)
                            )
        for c in stores(n):
            c.start()
    for n in range(len(units) - 2, len(units)):
        for c in stores(n):
            c.wait()


def contract(groups, gathered, pos, place, right, parts, base):
    ins = [pos, place, right, *parts]
    if base is not None:
        ins.append(base)
    units = 4 * len(groups)
    return pl.pallas_call(
        functools.partial(contract_kernel, groups, gathered),
        out_shape=arr(8192, 1024),
        in_specs=[SM, SM] + [ANY] * (len(ins) - 2),
        out_specs=ANY,
        scratch_shapes=[
            pltpu.VMEM((KF, 1024), BF),
            pltpu.VMEM((units, 8, 4, UR, KF), BF),
            pltpu.VMEM((2, 4, 128, 1024), BF),
            pltpu.SemaphoreType.DMA,
            pltpu.SemaphoreType.DMA((units, 2)),
            pltpu.SemaphoreType.DMA((2, 4)),
        ],
        input_output_aliases={} if base is None else {len(ins) - 1: 0},
        compiler_params=pltpu.CompilerParams(vmem_limit_bytes=56 << 20),
        cost_estimate=cost(2 * units * 512 * KF * 1024, units * 512 * (KF + 1024) * 2),
    )(*ins)


def after(value, *done):
    return lax.optimization_barrier((value, *done))[0]


def local(coupling, right_coupling, upper_inverse, lower_inverse, block_mask, block_map):
    row, col = lax.axis_index("row"), lax.axis_index("col")
    pos = jnp.stack([row, col]).astype(jnp.int32)

    here = lax.dynamic_slice_in_dim(block_map, row * 64, 64) - row * 64
    slots = jnp.arange(64, dtype=jnp.int32)
    place = jnp.sum(
        jnp.where(here[None, :] == slots[:, None], slots[None, :], 0), axis=1, dtype=jnp.int32
    )

    a, b = solve(block_mask, coupling, upper_inverse)
    b_below, b_above, b_far = shift(b, dy=1), shift(b, dy=-1), shift(b, dy=2)
    own, b_below, b_above, b_far = lax.optimization_barrier(
        (exchange(a, XZ).reshape(4, 4, 3, UR, KF), b_below, b_above, b_far)
    )

    whole = lax.all_gather(own, "col", axis=0, tiled=False, axis_index_groups=YC)
    raw = after(right_coupling.reshape(KF, 128), own)
    w_other = permute(raw, lambda x, y, z, c: (x, y, z ^ 1, c))
    by = after_y(pos, b, b_below, b_above, b_far)
    bx, w_other = lax.optimization_barrier((exchange(by, XX), w_other))
    pair = stack(raw, w_other)
    bz, pair = lax.optimization_barrier((after_x(bx), pair))
    zs = exchange(bz, ZZ)
    w_below, w_above, w_far = shift(pair, dx=1), shift(pair, dx=-1), shift(pair, dx=2)
    zs, w_below, w_above, w_far = lax.optimization_barrier((zs, w_below, w_above, w_far))
    right = window(pos, [pair, w_below, w_above, w_far], lower_inverse)
    out = contract((3,), False, pos, place, right, [zs, shift(zs, dc=1)], None)
    return contract((0, 1, 2), True, pos, place, right, [whole], out)


def solution(mesh):
    placed = (
        P(None, None, ("row", "col")),
        P(None, None, ("col", "row")),
        P(),
        P(),
        P(None, ("row", "col")),
        P(),
    )
    return jax.shard_map(
        local, mesh=mesh, in_specs=placed, out_specs=P("row", "col"), check_vma=False
    )
```

```python
import functools

import jax
import jax.numpy as jnp
from jax import lax
from jax.experimental import pallas as pl
from jax.experimental.pallas import tpu as pltpu
from jax.sharding import PartitionSpec as P

BF = jnp.bfloat16
F32 = jnp.float32
AXES = ("row", "col")
KF = 768
DEPTH = 4
UR = 16
ANY = pl.BlockSpec(memory_space=pl.ANY)
VM = pl.BlockSpec(memory_space=pltpu.VMEM)
SM = pl.BlockSpec(memory_space=pltpu.SMEM)


def coords(d):
    row, col = divmod(d, 16)
    x, zl = divmod(row, 2)
    y, rest = divmod(col, 4)
    zh, core = divmod(rest, 2)
    return x, y, zh * 2 + zl, core


def linear(x, y, z, core):
    x, y, z = x % 4, y % 4, z % 4
    return (x * 2 + z % 2) * 16 + y * 4 + (z // 2) * 2 + core


def permute(a, to):
    return lax.ppermute(a, AXES, [(d, linear(*to(*coords(d)))) for d in range(128)])


def shift(a, dx=0, dy=0, dz=0, dc=0):
    return permute(a, lambda x, y, z, c: (x + dx, y + dy, z + dz, c ^ dc))


R4 = range(4)
XZ = [[linear(x, y, z, c) for x in R4 for z in R4] for y in R4 for c in (0, 1)]
XX = [[linear(x, y, z, c) for x in R4] for y in R4 for z in R4 for c in (0, 1)]
YC = [[y * 4 + zh * 2 + c for y in R4 for c in (0, 1)] for zh in (0, 1)]
ZZ = [[linear(x, y, z, c) for z in R4] for x in R4 for y in R4 for c in (0, 1)]


def exchange(a, groups):
    return lax.all_to_all(a, AXES, split_axis=0, concat_axis=0, tiled=True, axis_index_groups=groups)


def arr(*shape, dtype=BF):
    return jax.ShapeDtypeStruct(shape, dtype)


def cost(flops, nbytes):
    return pl.CostEstimate(flops=flops, bytes_accessed=nbytes, transcendentals=0)


def place_of(pos):
    row, col = pos[0], pos[1]
    return row // 2, col // 4, (col // 2) % 2 * 2 + row % 2, col % 2


def run(copies):
    for c in copies:
        c.start()
    for c in copies:
        c.wait()


def solve_kernel(mask, coupling, upper, a, b, c_v, u_v, hold, sem):
    copies = []
    for k in range(3):
        copies.append(pltpu.make_async_copy(coupling.at[k], c_v.at[k], sem.at[k, 0]))
        copies.append(pltpu.make_async_copy(upper.at[k], u_v.at[k], sem.at[k, 1]))
    for c in copies:
        c.start()
    for k in range(3):
        copies[2 * k].wait()
        copies[2 * k + 1].wait()
        row = jnp.concatenate(
            [jnp.broadcast_to(mask[k : k + 1, j : j + 1], (1, 128)) for j in range(4)], axis=1
        )
        masked = c_v[k] * row.astype(F32).astype(BF)
        solved = lax.dot_general(
            masked, u_v[k], (((0,), (0,)), ((), ())), preferred_element_type=F32
        )
        hold[:, :, :, k * 256 : (k + 1) * 256] = solved.astype(BF).reshape(8, 4, UR, 256)
    for to in range(16):
        target = to // 4 * 2 + to % 2
        a[to] = hold[target, 0:3]
    for x in range(4):
        for zl in range(2):
            b[x, zl] = hold[x * 2 + zl, 3]


def solve(mask, coupling, upper):
    return pl.pallas_call(
        solve_kernel,
        out_shape=(arr(16, 3, UR, KF), arr(4, 2, UR, KF)),
        in_specs=[VM, ANY, ANY],
        out_specs=(VM,) * 2,
        scratch_shapes=[
            pltpu.VMEM((3, 256, 512), BF),
            pltpu.VMEM((3, 256, 256), BF),
            pltpu.VMEM((8, 4, UR, KF), BF),
            pltpu.SemaphoreType.DMA((3, 2)),
        ],
        compiler_params=pltpu.CompilerParams(vmem_limit_bytes=60 << 20),
        cost_estimate=cost(2 * 512 * 256 * 768, 4 << 20),
    )(mask, coupling, upper)


def after_y_kernel(pos, own, below, above, far, out):
    _, y, _, _ = place_of(pos)
    for dy, src in ((0, own), (3, below), (1, above), (2, far)):
        for x in range(4):
            out[x, lax.rem(y + dy, 4)] = src[x]


def after_y(pos, *parts):
    return pl.pallas_call(
        after_y_kernel,
        out_shape=arr(4, 4, 2, UR, KF),
        in_specs=[SM] + [VM] * 4,
        out_specs=VM,
        compiler_params=pltpu.CompilerParams(vmem_limit_bytes=4 << 20),
        cost_estimate=cost(0, 2 << 20),
    )(pos, *parts)


def after_x_kernel(got, out):
    for z in range(4):
        for x in range(4):
            for y in range(4):
                out[z, x, y] = got[x, y, z % 2]


def after_x(got):
    return pl.pallas_call(
        after_x_kernel,
        out_shape=arr(4, 4, 4, UR, KF),
        in_specs=[VM],
        out_specs=VM,
        compiler_params=pltpu.CompilerParams(vmem_limit_bytes=4 << 20),
        cost_estimate=cost(0, 3 << 20),
    )(got)


def move_kernel(where, *refs):
    ins, outs = refs[: -len(where)], refs[-len(where) :]
    for out, pieces in zip(outs, where):
        for to, (i, at) in enumerate(pieces):
            out[to] = ins[i][at]


def move(where, shapes, *ins):
    return pl.pallas_call(
        functools.partial(move_kernel, where),
        out_shape=tuple(arr(*s) for s in shapes),
        in_specs=[VM] * len(ins),
        out_specs=(VM,) * len(where),
        compiler_params=pltpu.CompilerParams(vmem_limit_bytes=4 << 20),
        cost_estimate=cost(0, 1 << 20),
    )(*ins)


def stack(a, b):
    return move(([(0, ...), (1, ...)],), ((2, KF, 128),), a, b)[0]


def window_kernel(pos, own, below, above, far, lower, out, right):
    x, _, z, _ = place_of(pos)
    for dx, src in ((0, own), (3, below), (1, above), (2, far)):
        for e in range(2):
            r = lax.rem(x + dx, 4) * 2 + lax.rem(z + e, 2)
            right[:, pl.ds(pl.multiple_of(r * 128, 128), 128)] = src[e]
    for k in range(3):
        rows = slice(k * 256, (k + 1) * 256)
        solved = jnp.dot(lower[k], right[rows], preferred_element_type=F32)
        out[rows] = (-solved).astype(BF)


def window(pos, parts, lower):
    return pl.pallas_call(
        window_kernel,
        out_shape=arr(KF, 1024),
        in_specs=[SM] + [VM] * 5,
        out_specs=VM,
        scratch_shapes=[pltpu.VMEM((KF, 1024), BF)],
        compiler_params=pltpu.CompilerParams(vmem_limit_bytes=16 << 20),
        cost_estimate=cost(2 * 768 * 256 * 1024, 4 << 20),
    )(pos, *parts, lower)


def contract_kernel(groups, gathered, *refs):
    pos, place, right = refs[:3]
    out, right_v, left, stage, r_sem, in_sem, out_sem = refs[-7:]
    _, _, _, core = place_of(pos)
    right_in = pltpu.make_async_copy(right, right_v, r_sem)
    units = [(u, i) for u in range(4) for i in range(len(groups))]

    def loads(n):
        u, i = units[n]
        if gathered:
            pairs = [(refs[3].at[:, u, :, i], left.at[n])]
        else:
            pairs = [
                (refs[3].at[:, u], left.at[n, pl.ds(core * 4, 4)]),
                (refs[4].at[:, u], left.at[n, pl.ds((1 - core) * 4, 4)]),
            ]
        return [
            pltpu.make_async_copy(src, dst, in_sem.at[n, k]) for k, (src, dst) in enumerate(pairs)
        ]

    def stores(n):
        u, i = units[n]
        made = []
        for p in range(4):
            at = place[(groups[i] * 4 + p) * 4 + u]
            rows = pl.ds(pl.multiple_of(at * 128, 128), 128)
            made.append(pltpu.make_async_copy(stage.at[n % 4, p], out.at[rows], out_sem.at[n % 4, p]))
        return made

    for c in loads(0):
        c.start()
    right_in.start()
    for n in range(1, DEPTH):
        for c in loads(n):
            c.start()
    right_in.wait()
    low = lax.broadcasted_iota(jnp.int32, (1, 1, 8, 256), 2) < 4
    for n0 in range(0, len(units), 2):
        for n in range(n0, n0 + 2):
            for c in loads(n):
                c.wait()
            if n + DEPTH < len(units):
                for c in loads(n + DEPTH):
                    c.start()
            if n >= 4:
                for c in stores(n - 4):
                    c.wait()
        flat = left[n0 : n0 + 2].reshape(2 * 512, KF)
        for j in range(4):
            cols = slice(j * 256, (j + 1) * 256)
            whole = jnp.dot(flat, right_v[:, cols], preferred_element_type=F32)
            for n in range(n0, n0 + 2):
                acc = whole[(n - n0) * 512 : (n - n0 + 1) * 512]
                if gathered:
                    acc = acc.reshape(4, 2, 4, 2, 8, 256)
                    c0, c1 = acc[:, 0].reshape(16, 2, 8, 256), acc[:, 1].reshape(16, 2, 8, 256)
                else:
                    acc = acc.reshape(2, 16, 2, 8, 256)
                    c0, c1 = acc[0], acc[1]
                even = jnp.where(low, c0, pltpu.roll(c1, 4, 2))
                odd = jnp.where(low, pltpu.roll(c0, 4, 2), c1)
                for half, made in enumerate((even, odd)):
                    for pair in range(2):
                        for y in range(4):
                            for zl in range(2):
                                at = [
                                    made[y * 4 + z if gathered else z * 4 + y, pair]
                                    for z in (zl, zl + 2)
                                ]
                                r0 = (zl * 4 + y) * 16
                                stage[n % 4, pair * 2 + half, r0 : r0 + 16, cols] = (
                                    jnp.concatenate(at, axis=0).astype(BF)
                                )
                if j == 3:
                    for c in stores(n):
                        c.start()
    for n in range(max(0, len(units) - 4), len(units)):
        for c in stores(n):
            c.wait()


def contract(groups, gathered, pos, place, right, parts, base):
    ins = [pos, place, right, *parts]
    if base is not None:
        ins.append(base)
    units = 4 * len(groups)
    return pl.pallas_call(
        functools.partial(contract_kernel, groups, gathered),
        out_shape=arr(8192, 1024),
        in_specs=[SM, SM] + [ANY] * (len(ins) - 2),
        out_specs=ANY,
        scratch_shapes=[
            pltpu.VMEM((KF, 1024), BF),
            pltpu.VMEM((units, 8, 4, UR, KF), BF),
            pltpu.VMEM((4, 4, 128, 1024), BF),
            pltpu.SemaphoreType.DMA,
            pltpu.SemaphoreType.DMA((units, 2)),
            pltpu.SemaphoreType.DMA((4, 4)),
        ],
        input_output_aliases={} if base is None else {len(ins) - 1: 0},
        compiler_params=pltpu.CompilerParams(vmem_limit_bytes=56 << 20),
        cost_estimate=cost(2 * units * 512 * KF * 1024, units * 512 * (KF + 1024) * 2),
    )(*ins)


def after(value, *done):
    return lax.optimization_barrier((value, *done))[0]


def local(coupling, right_coupling, upper_inverse, lower_inverse, block_mask, block_map):
    row, col = lax.axis_index("row"), lax.axis_index("col")
    pos = jnp.stack([row, col]).astype(jnp.int32)

    here = lax.dynamic_slice_in_dim(block_map, row * 64, 64) - row * 64
    slots = jnp.arange(64, dtype=jnp.int32)
    place = jnp.sum(
        jnp.where(here[None, :] == slots[:, None], slots[None, :], 0), axis=1, dtype=jnp.int32
    )

    a, b = solve(block_mask, coupling, upper_inverse)
    b_below, b_above, b_far = shift(b, dy=1), shift(b, dy=-1), shift(b, dy=2)
    own, b_below, b_above, b_far = lax.optimization_barrier(
        (exchange(a, XZ).reshape(4, 4, 3, UR, KF), b_below, b_above, b_far)
    )

    whole = lax.all_gather(own, "col", axis=0, tiled=False, axis_index_groups=YC)
    raw = after(right_coupling.reshape(KF, 128), own)
    w_other = permute(raw, lambda x, y, z, c: (x, y, z ^ 1, c))
    by = after_y(pos, b, b_below, b_above, b_far)
    bx, w_other = lax.optimization_barrier((exchange(by, XX), w_other))
    pair = stack(raw, w_other)
    bz, pair = lax.optimization_barrier((after_x(bx), pair))
    zs = exchange(bz, ZZ)
    w_below, w_above, w_far = shift(pair, dx=1), shift(pair, dx=-1), shift(pair, dx=2)
    zs, w_below, w_above, w_far = lax.optimization_barrier((zs, w_below, w_above, w_far))
    right = window(pos, [pair, w_below, w_above, w_far], lower_inverse)
    out = contract((3,), False, pos, place, right, [zs, shift(zs, dc=1)], None)
    return contract((0, 1, 2), True, pos, place, right, [whole], out)


def solution(mesh):
    placed = (
        P(None, None, ("row", "col")),
        P(None, None, ("col", "row")),
        P(),
        P(),
        P(None, ("row", "col")),
        P(),
    )
    return jax.shard_map(
        local, mesh=mesh, in_specs=placed, out_specs=P("row", "col"), check_vma=False
    )
```

```python
import functools

import jax
import jax.numpy as jnp
from jax import lax
from jax.experimental import pallas as pl
from jax.experimental.pallas import tpu as pltpu
from jax.sharding import PartitionSpec as P

BF = jnp.bfloat16
F32 = jnp.float32
AXES = ("row", "col")
KF = 768
DEPTH = 4
UR = 16
ANY = pl.BlockSpec(memory_space=pl.ANY)
VM = pl.BlockSpec(memory_space=pltpu.VMEM)
SM = pl.BlockSpec(memory_space=pltpu.SMEM)


def coords(d):
    row, col = divmod(d, 16)
    x, zl = divmod(row, 2)
    y, rest = divmod(col, 4)
    zh, core = divmod(rest, 2)
    return x, y, zh * 2 + zl, core


def linear(x, y, z, core):
    x, y, z = x % 4, y % 4, z % 4
    return (x * 2 + z % 2) * 16 + y * 4 + (z // 2) * 2 + core


def permute(a, to):
    return lax.ppermute(a, AXES, [(d, linear(*to(*coords(d)))) for d in range(128)])


def shift(a, dx=0, dy=0, dz=0, dc=0):
    return permute(a, lambda x, y, z, c: (x + dx, y + dy, z + dz, c ^ dc))


R4 = range(4)
XZ = [[linear(x, y, z, c) for x in R4 for z in R4] for y in R4 for c in (0, 1)]
XX = [[linear(x, y, z, c) for x in R4] for y in R4 for z in R4 for c in (0, 1)]
YC = [[y * 4 + zh * 2 + c for y in R4 for c in (0, 1)] for zh in (0, 1)]
ZZ = [[linear(x, y, z, c) for z in R4] for x in R4 for y in R4 for c in (0, 1)]


def exchange(a, groups):
    return lax.all_to_all(a, AXES, split_axis=0, concat_axis=0, tiled=True, axis_index_groups=groups)


def arr(*shape, dtype=BF):
    return jax.ShapeDtypeStruct(shape, dtype)


def cost(flops, nbytes):
    return pl.CostEstimate(flops=flops, bytes_accessed=nbytes, transcendentals=0)


def place_of(pos):
    row, col = pos[0], pos[1]
    return row // 2, col // 4, (col // 2) % 2 * 2 + row % 2, col % 2


def run(copies):
    for c in copies:
        c.start()
    for c in copies:
        c.wait()


def solve_kernel(mask, coupling, upper, a, b, c_v, u_v, hold, sem):
    copies = []
    for k in range(3):
        copies.append(pltpu.make_async_copy(coupling.at[k], c_v.at[k], sem.at[k, 0]))
        copies.append(pltpu.make_async_copy(upper.at[k], u_v.at[k], sem.at[k, 1]))
    for c in copies:
        c.start()
    for k in range(3):
        copies[2 * k].wait()
        copies[2 * k + 1].wait()
        row = jnp.concatenate(
            [jnp.broadcast_to(mask[k : k + 1, j : j + 1], (1, 128)) for j in range(4)], axis=1
        )
        masked = c_v[k] * row.astype(F32).astype(BF)
        solved = lax.dot_general(
            masked, u_v[k], (((0,), (0,)), ((), ())), preferred_element_type=F32
        )
        hold[:, :, :, k * 256 : (k + 1) * 256] = solved.astype(BF).reshape(8, 4, UR, 256)
    for to in range(16):
        target = to // 4 * 2 + to % 2
        a[to] = hold[target, 0:3]
    for x in range(4):
        for zl in range(2):
            b[x, zl] = hold[x * 2 + zl, 3]


def solve(mask, coupling, upper):
    return pl.pallas_call(
        solve_kernel,
        out_shape=(arr(16, 3, UR, KF), arr(4, 2, UR, KF)),
        in_specs=[VM, ANY, ANY],
        out_specs=(VM,) * 2,
        scratch_shapes=[
            pltpu.VMEM((3, 256, 512), BF),
            pltpu.VMEM((3, 256, 256), BF),
            pltpu.VMEM((8, 4, UR, KF), BF),
            pltpu.SemaphoreType.DMA((3, 2)),
        ],
        compiler_params=pltpu.CompilerParams(vmem_limit_bytes=60 << 20),
        cost_estimate=cost(2 * 512 * 256 * 768, 4 << 20),
    )(mask, coupling, upper)


def after_y_kernel(pos, own, below, above, far, out):
    _, y, _, _ = place_of(pos)
    for dy, src in ((0, own), (3, below), (1, above), (2, far)):
        for x in range(4):
            out[x, lax.rem(y + dy, 4)] = src[x]


def after_y(pos, *parts):
    return pl.pallas_call(
        after_y_kernel,
        out_shape=arr(4, 4, 2, UR, KF),
        in_specs=[SM] + [VM] * 4,
        out_specs=VM,
        compiler_params=pltpu.CompilerParams(vmem_limit_bytes=4 << 20),
        cost_estimate=cost(0, 2 << 20),
    )(pos, *parts)


def after_x_kernel(got, out):
    for z in range(4):
        for x in range(4):
            for y in range(4):
                out[z, x, y] = got[x, y, z % 2]


def after_x(got):
    return pl.pallas_call(
        after_x_kernel,
        out_shape=arr(4, 4, 4, UR, KF),
        in_specs=[VM],
        out_specs=VM,
        compiler_params=pltpu.CompilerParams(vmem_limit_bytes=4 << 20),
        cost_estimate=cost(0, 3 << 20),
    )(got)


def move_kernel(where, *refs):
    ins, outs = refs[: -len(where)], refs[-len(where) :]
    for out, pieces in zip(outs, where):
        for to, (i, at) in enumerate(pieces):
            out[to] = ins[i][at]


def move(where, shapes, *ins):
    return pl.pallas_call(
        functools.partial(move_kernel, where),
        out_shape=tuple(arr(*s) for s in shapes),
        in_specs=[VM] * len(ins),
        out_specs=(VM,) * len(where),
        compiler_params=pltpu.CompilerParams(vmem_limit_bytes=4 << 20),
        cost_estimate=cost(0, 1 << 20),
    )(*ins)


def stack(a, b):
    return move(([(0, ...), (1, ...)],), ((2, KF, 128),), a, b)[0]


def window_kernel(pos, own, below, above, far, lower, out, right):
    x, _, z, _ = place_of(pos)
    for dx, src in ((0, own), (3, below), (1, above), (2, far)):
        for e in range(2):
            r = lax.rem(x + dx, 4) * 2 + lax.rem(z + e, 2)
            right[:, pl.ds(pl.multiple_of(r * 128, 128), 128)] = src[e]
    for k in range(3):
        rows = slice(k * 256, (k + 1) * 256)
        solved = jnp.dot(lower[k], right[rows], preferred_element_type=F32)
        out[rows] = (-solved).astype(BF)


def window(pos, parts, lower):
    return pl.pallas_call(
        window_kernel,
        out_shape=arr(KF, 1024),
        in_specs=[SM] + [VM] * 5,
        out_specs=VM,
        scratch_shapes=[pltpu.VMEM((KF, 1024), BF)],
        compiler_params=pltpu.CompilerParams(vmem_limit_bytes=16 << 20),
        cost_estimate=cost(2 * 768 * 256 * 1024, 4 << 20),
    )(pos, *parts, lower)


def contract_kernel(groups, gathered, *refs):
    pos, place, right = refs[:3]
    out, right_v, left, stage, r_sem, in_sem, out_sem = refs[-7:]
    _, _, _, core = place_of(pos)
    right_in = pltpu.make_async_copy(right, right_v, r_sem)
    units = [(u, i) for u in range(4) for i in range(len(groups))]

    def loads(n):
        u, i = units[n]
        if gathered:
            pairs = [(refs[3].at[:, u, :, i], left.at[n])]
        else:
            pairs = [
                (refs[3].at[:, u], left.at[n, pl.ds(core * 4, 4)]),
                (refs[4].at[:, u], left.at[n, pl.ds((1 - core) * 4, 4)]),
            ]
        return [
            pltpu.make_async_copy(src, dst, in_sem.at[n, k]) for k, (src, dst) in enumerate(pairs)
        ]

    def stores(n, cols=slice(0, 1024)):
        u, i = units[n]
        made = []
        span = pl.ds(cols.start, cols.stop - cols.start)
        for p in range(4):
            at = place[(groups[i] * 4 + p) * 4 + u]
            rows = pl.ds(pl.multiple_of(at * 128, 128), 128)
            made.append(
                pltpu.make_async_copy(
                    stage.at[n % 4, p, :, span],
                    out.at[rows, span],
                    out_sem.at[n % 4, p, cols.start // 256],
                )
            )
        return made

    for c in loads(0):
        c.start()
    right_in.start()
    for n in range(1, DEPTH):
        for c in loads(n):
            c.start()
    right_in.wait()
    low = lax.broadcasted_iota(jnp.int32, (1, 1, 8, 256), 2) < 4
    for n0 in range(0, len(units), 2):
        for n in range(n0, n0 + 2):
            for c in loads(n):
                c.wait()
            if n + DEPTH < len(units):
                for c in loads(n + DEPTH):
                    c.start()
            if n >= 4:
                for c in stores(n - 4):
                    c.wait()
        flat = left[n0 : n0 + 2].reshape(2 * 512, KF)
        for j in range(4):
            cols = slice(j * 256, (j + 1) * 256)
            whole = jnp.dot(flat, right_v[:, cols], preferred_element_type=F32)
            for n in range(n0, n0 + 2):
                acc = whole[(n - n0) * 512 : (n - n0 + 1) * 512]
                if gathered:
                    acc = acc.reshape(4, 2, 4, 2, 8, 256)
                    c0, c1 = acc[:, 0].reshape(16, 2, 8, 256), acc[:, 1].reshape(16, 2, 8, 256)
                else:
                    acc = acc.reshape(2, 16, 2, 8, 256)
                    c0, c1 = acc[0], acc[1]
                even = jnp.where(low, c0, pltpu.roll(c1, 4, 2))
                odd = jnp.where(low, pltpu.roll(c0, 4, 2), c1)
                for half, made in enumerate((even, odd)):
                    for pair in range(2):
                        for y in range(4):
                            for zl in range(2):
                                at = [
                                    made[y * 4 + z if gathered else z * 4 + y, pair]
                                    for z in (zl, zl + 2)
                                ]
                                r0 = (zl * 4 + y) * 16
                                stage[n % 4, pair * 2 + half, r0 : r0 + 16, cols] = (
                                    jnp.concatenate(at, axis=0).astype(BF)
                                )
                if n >= len(units) - 2:
                    for c in stores(n, cols):
                        c.start()
                elif j == 3:
                    for c in stores(n):
                        c.start()
    for n in range(len(units) - 4, len(units) - 2):
        for c in stores(n):
            c.wait()
    for n in range(len(units) - 2, len(units)):
        for j in range(4):
            for c in stores(n, slice(j * 256, (j + 1) * 256)):
                c.wait()


def contract(groups, gathered, pos, place, right, parts, base):
    ins = [pos, place, right, *parts]
    if base is not None:
        ins.append(base)
    units = 4 * len(groups)
    return pl.pallas_call(
        functools.partial(contract_kernel, groups, gathered),
        out_shape=arr(8192, 1024),
        in_specs=[SM, SM] + [ANY] * (len(ins) - 2),
        out_specs=ANY,
        scratch_shapes=[
            pltpu.VMEM((KF, 1024), BF),
            pltpu.VMEM((units, 8, 4, UR, KF), BF),
            pltpu.VMEM((4, 4, 128, 1024), BF),
            pltpu.SemaphoreType.DMA,
            pltpu.SemaphoreType.DMA((units, 2)),
            pltpu.SemaphoreType.DMA((4, 4, 4)),
        ],
        input_output_aliases={} if base is None else {len(ins) - 1: 0},
        compiler_params=pltpu.CompilerParams(vmem_limit_bytes=56 << 20),
        cost_estimate=cost(2 * units * 512 * KF * 1024, units * 512 * (KF + 1024) * 2),
    )(*ins)


def after(value, *done):
    return lax.optimization_barrier((value, *done))[0]


def local(coupling, right_coupling, upper_inverse, lower_inverse, block_mask, block_map):
    row, col = lax.axis_index("row"), lax.axis_index("col")
    pos = jnp.stack([row, col]).astype(jnp.int32)

    here = lax.dynamic_slice_in_dim(block_map, row * 64, 64) - row * 64
    slots = jnp.arange(64, dtype=jnp.int32)
    place = jnp.sum(
        jnp.where(here[None, :] == slots[:, None], slots[None, :], 0), axis=1, dtype=jnp.int32
    )

    a, b = solve(block_mask, coupling, upper_inverse)
    b_below, b_above, b_far = shift(b, dy=1), shift(b, dy=-1), shift(b, dy=2)
    own, b_below, b_above, b_far = lax.optimization_barrier(
        (exchange(a, XZ).reshape(4, 4, 3, UR, KF), b_below, b_above, b_far)
    )

    whole = lax.all_gather(own, "col", axis=0, tiled=False, axis_index_groups=YC)
    raw = after(right_coupling.reshape(KF, 128), own)
    w_other = permute(raw, lambda x, y, z, c: (x, y, z ^ 1, c))
    by = after_y(pos, b, b_below, b_above, b_far)
    bx, w_other = lax.optimization_barrier((exchange(by, XX), w_other))
    pair = stack(raw, w_other)
    bz, pair = lax.optimization_barrier((after_x(bx), pair))
    zs = exchange(bz, ZZ)
    w_below, w_above, w_far = shift(pair, dx=1), shift(pair, dx=-1), shift(pair, dx=2)
    zs, w_below, w_above, w_far = lax.optimization_barrier((zs, w_below, w_above, w_far))
    right = window(pos, [pair, w_below, w_above, w_far], lower_inverse)
    out = contract((3,), False, pos, place, right, [zs, shift(zs, dc=1)], None)
    return contract((0, 1, 2), True, pos, place, right, [whole], out)


def solution(mesh):
    placed = (
        P(None, None, ("row", "col")),
        P(None, None, ("col", "row")),
        P(),
        P(),
        P(None, ("row", "col")),
        P(),
    )
    return jax.shard_map(
        local, mesh=mesh, in_specs=placed, out_specs=P("row", "col"), check_vma=False
    )
```
